512 devices in a mesh: blk: 128 (over x, z_lo, y), probe: 4 (over z_hi, core).
Axes of the slice: x: 4, y: 4, z: 16 (z_hi: 2, z_lo: 8; z = z_hi * 8 + z_lo), core: 2. Of those that a mesh axis runs over, the one named last changes fastest.
Arguments:
- positions: bfloat16 [3, 4096], P(None, 'blk'), may hold values from 0 to 4
- scales: bfloat16 [4096], P('blk'), may hold values from 0.5 to 2
- onsite: float32 [4096], P('blk'), may hold values from 0.5 to 1.5
- probes: bfloat16 [3, 64, 4096], P(None, 'probe', 'blk'), may hold values from -4 to 4
Outputs:
- chebyshev_two: float32 [3, 64, 4096], P(None, 'probe', 'blk')
- forces: float32 [3, 4096], P(None, 'blk')
- energy: float32 [], replicated
The draws below stay inside these ranges and needn't reach their ends.
All inputs are finite; a program needn't handle non-finite values.
Results may differ from the reference program's by a relative error of at most 0.0015.
Values may be sent and summed in bfloat16 or wider, within the bound.
No kernel may reach another device: no remote copies, remote signals or barrier semaphores. Data moves between devices by JAX's collectives and lax.ppermute only.
A program may use at most 64 MiB of HBM per device.

```python
import math
import jax
import jax.numpy as jnp
from jax import lax

ATOM_DEV = 32
PROBES = 64
ATOMS = 4096


def shard_levels(rng, dims, shards, low, high):
    def one(dim, parts):
        draws = jax.random.uniform(jax.random.fold_in(jax.random.fold_in(rng, 6), dim), (parts,), jnp.float32, low / len(shards), high / len(shards))
        return jnp.repeat(jnp.exp(draws), dims[dim] // parts).reshape((-1,) + (1,) * (len(dims) - dim - 1))

    level = one(*shards[0])
    for cut in shards[1:]:
        level = level * one(*cut)
    return level


def bell_draw(own_key, dims, width, bound, pieces=(), kind=jnp.bfloat16):
    result = jax.random.normal(own_key, dims, jnp.float32) * width
    if len(pieces) > 0:
        result = shard_levels(own_key, dims, pieces, -0.22, 0.18) * result
    return jnp.clip(result, min=-bound, max=bound).astype(kind)


def setup_inputs(seed: int = 0) -> dict:
    splits = jax.random.split(jax.random.key(seed), 5)
    positions = jnp.clip(4.0 * jax.random.uniform(splits[0], (3, ATOMS), jnp.float32) ** shard_levels(splits[0], (3, ATOMS), ((1, 128),), -0.2, 0.2), 0.0, 4.0).astype(jnp.bfloat16)
    scales = jnp.clip(jnp.exp(math.log(2.0) - 1.3862944 * jax.random.uniform(splits[1], (ATOMS,), jnp.float32) ** shard_levels(splits[1], (ATOMS,), ((0, 128),), -0.2, 0.2)), 0.5, 2.0).astype(jnp.bfloat16)
    onsite = jnp.clip(0.5 + 1.0 * jax.random.uniform(splits[2], (ATOMS,), jnp.float32) ** shard_levels(splits[2], (ATOMS,), ((0, 128),), -0.2, 0.2), 0.5, 1.5)
    probes = bell_draw(splits[3], (3, PROBES, ATOMS), 1.0, 4.0, ((1, 4), (2, 128)))
    return {"positions": positions, "scales": scales, "onsite": onsite, "probes": probes}


SOFTENING = 0.5

def couple(row_coords, row_charges, col_coords, col_charges, row_ids, col_ids, strength):
    offset_vec = row_coords[:, :, None] - col_coords[:, None, :]
    dist_sq = lax.optimization_barrier(jnp.sum(offset_vec * offset_vec, axis=0)) + SOFTENING * SOFTENING
    inverse = lax.rsqrt(dist_sq)
    inv_cube = inverse * inverse * inverse
    inv_five = inv_cube * inverse * inverse
    keep_mask = jnp.where(row_ids[:, None] == col_ids[None, :], 0.0, 1.0).astype(row_coords.dtype)
    scaling = strength * row_charges[:, None] * col_charges[None, :] * keep_mask
    identity = jnp.eye(3, dtype=row_coords.dtype)
    tensor = 3.0 * offset_vec[:, None] * offset_vec[None, :] * inv_five - identity[:, :, None, None] * inv_cube
    return tensor * scaling

def reference(positions, scales, onsite, probes):
    coords = positions.astype(jnp.float32)
    charges = scales.astype(jnp.float32)
    atom_ids = jnp.arange(ATOMS, dtype=jnp.int32)
    strength = 4.0 / math.sqrt(ATOMS)
    block_count = ATOMS // ATOM_DEV
    starts = jnp.arange(block_count, dtype=jnp.int32) * ATOM_DEV

    def row_slice(array, start_row):
        return lax.dynamic_slice_in_dim(array, start_row, ATOM_DEV, array.ndim - 1)

    def apply_matrix(vectors):
        wide = vectors.astype(jnp.float32)

        def row_block(start_row):
            tile_mat = couple(row_slice(coords, start_row), row_slice(charges, start_row), coords, charges, row_slice(atom_ids, start_row), atom_ids, strength)
            rounded = lax.optimization_barrier(tile_mat.astype(jnp.bfloat16))
            return jnp.einsum('cdij,dpj->cpi', rounded.astype(jnp.float32), wide, precision=lax.Precision.HIGHEST)
        blocks = lax.map(row_block, starts)
        return jnp.transpose(blocks, (1, 2, 0, 3)).reshape(3, PROBES, ATOMS)
    probe_wide = probes.astype(jnp.float32)
    step_one = (onsite * probe_wide + apply_matrix(probes)).astype(jnp.bfloat16)
    step_wide = step_one.astype(jnp.float32)
    chebyshev_two = 2.0 * (onsite * step_wide + apply_matrix(step_one)) - probe_wide
    energy = (0.5 * jnp.sum(probe_wide * step_wide) - 0.25 * jnp.sum(probe_wide * chebyshev_two)) / PROBES

    def force_block(start_row):
        probe_rows = row_slice(probe_wide, start_row)
        step_rows = row_slice(step_wide, start_row)
        weight = 0.5 * jnp.einsum('cpi,dpj->cdij', probe_rows, probe_wide - step_wide, precision=lax.Precision.HIGHEST)
        weight = weight - 0.5 * jnp.einsum('cpi,dpj->cdij', step_rows, probe_wide, precision=lax.Precision.HIGHEST)

        def tile_of(row_coords):
            return couple(row_coords, row_slice(charges, start_row), coords, charges, row_slice(atom_ids, start_row), atom_ids, strength)
        unused, pull_back = jax.vjp(tile_of, row_slice(coords, start_row))
        return pull_back(weight)[0]
    grads = lax.map(force_block, starts)
    forces = -(2.0 / PROBES) * jnp.transpose(grads, (1, 0, 2)).reshape(3, ATOMS)
    return (chebyshev_two, forces, energy)
```

```python
import math

import jax
import jax.numpy as jnp
from jax import lax
from jax.experimental import pallas as pl
from jax.experimental.pallas import tpu as pltpu
from jax.sharding import Mesh, PartitionSpec as P

SOFT_SQ = 0.25
F32 = jnp.float32
BF16 = jnp.bfloat16

NX, NZL, NY, NZH, NC = 4, 8, 4, 2, 2
PLANE = NX * NY
LINE = NZL * NZH
A = 32
NP = 16
CH = NZL * A
PR = NZH * NP
VEC = 3 * PR
ROWS = VEC + 16
VMEM = 48 * 1024 * 1024


def split3(value):
    hi = value.astype(BF16)
    rest = value - hi.astype(F32)
    mid = rest.astype(BF16)
    low = (rest - mid.astype(F32)).astype(BF16)
    return hi.astype(F32), mid.astype(F32), low.astype(F32)


def pack_kernel(pos_ref, scale_ref, onsite_ref, probe_ref, out_ref):
    hi, mid, low = split3(onsite_ref[...])
    row = lax.broadcasted_iota(jnp.int32, (16, A), 0)
    meta = jnp.zeros((16, A), F32)
    pos = pos_ref[...].astype(F32)
    values = [pos[0:1], pos[1:2], pos[2:3], scale_ref[...].astype(F32), hi, mid, low]
    for k, value in enumerate(values):
        meta = jnp.where(row == k, jnp.broadcast_to(value, (16, A)), meta)
    parts = [probe_ref[c].astype(F32) for c in range(3)] + [meta]
    packet = jnp.concatenate(parts, axis=1).astype(BF16)
    for k in range(LINE):
        out_ref[k] = packet


def line_kernel(in_ref, out_ref):
    parts = []
    for q in range(3):
        for zh in range(NZH):
            parts.append(jnp.concatenate(
                [in_ref[zl * NZH + zh, :, q * A:(q + 1) * A] for zl in range(NZL)], axis=1))
    parts.append(jnp.concatenate(
        [in_ref[zl * NZH, :, 3 * A:4 * A] for zl in range(NZL)], axis=1))
    packet = jnp.concatenate(parts, axis=0)
    for k in range(PLANE):
        out_ref[k] = packet


def geometry(xi, yi, zi, si, xj, yj, zj, sj):
    rx, ry, rz = xi - xj, yi - yj, zi - zj
    q = lax.rsqrt(rx * rx + ry * ry + rz * rz + SOFT_SQ)
    q2 = q * q
    a = (si * sj) * (q2 * q)
    b = (3.0 * a) * q2
    return rx, ry, rz, q2, a, b


def tensor(rx, ry, rz, a, b):
    tx, ty, tz = rx * b, ry * b, rz * b
    return (tx * rx - a, tx * ry, tx * rz, ty * ry - a, ty * rz, tz * rz - a)


NT = (((1,), (1,)), ((), ()))


def columns(packet):
    wide = jnp.concatenate([packet.astype(F32), jnp.zeros((128 - ROWS, CH), F32)], axis=0)
    return wide.T


def step_kernel(ids, strength, far_ref, out_ref, tile_ref, col_ref, acc_ref):
    own = ids()[0]
    packet = far_ref[own]
    cols = columns(packet)
    for k in range(4):
        col_ref[k] = jnp.broadcast_to(cols[:, VEC + k:VEC + k + 1], (CH, 128))
    acc_ref[...] = jnp.zeros_like(acc_ref)
    sub = 32

    def chunk(jc, carry):
        meta = far_ref[jc, VEC:ROWS, :].astype(F32)
        for half in range(2):
            lanes = slice(half * 128, half * 128 + 128)
            xj, yj, zj = meta[0:1, lanes], meta[1:2, lanes], meta[2:3, lanes]
            sj = meta[3:4, lanes] * strength
            for i0 in range(0, CH, sub):
                rows = slice(i0, i0 + sub)
                rx, ry, rz, _, a, b = geometry(
                    col_ref[0, rows], col_ref[1, rows], col_ref[2, rows], col_ref[3, rows],
                    xj, yj, zj, sj)
                for k, value in enumerate(tensor(rx, ry, rz, a, b)):
                    tile_ref[k, rows, lanes] = value.astype(BF16)

        @pl.when(jc == own)
        def _():
            row = lax.broadcasted_iota(jnp.int32, (CH, CH), 0)
            col = lax.broadcasted_iota(jnp.int32, (CH, CH), 1)
            for k in range(6):
                kept = jnp.where(row == col, 0.0, tile_ref[k].astype(F32))
                tile_ref[k] = kept.astype(BF16)

        vec = far_ref[jc, 0:VEC, :]
        vx, vy, vz = vec[0:PR], vec[PR:2 * PR], vec[2 * PR:]

        def times(lhs, k):
            return lax.dot_general(lhs, tile_ref[k], NT, preferred_element_type=F32)

        xx, yy, zz = times(vx, 0), times(vy, 3), times(vz, 5)
        xy = times(vec[0:2 * PR], 1)
        yz = times(vec[PR:], 4)
        xz = times(jnp.concatenate([vx, vz], axis=0), 2)
        acc_ref[0:PR] += xx + xy[PR:] + xz[PR:]
        acc_ref[PR:2 * PR] += yy + xy[:PR] + yz[PR:]
        acc_ref[2 * PR:] += zz + xz[:PR] + yz[:PR]
        return carry

    lax.fori_loop(0, PLANE, chunk, 0)
    meta = packet[VEC:ROWS].astype(F32)
    onsite = meta[4:5] + meta[5:6] + meta[6:7]
    z = packet[0:VEC].astype(F32)
    exact = onsite * z + acc_ref[...]
    step = exact.astype(BF16)
    w = step.astype(F32)
    part = 0.5 * (z - exact) * w + 0.25 * z * z
    total = jnp.sum(jnp.sum(part, axis=0, keepdims=True), axis=1, keepdims=True)
    pieces = split3(total)
    row = lax.broadcasted_iota(jnp.int32, (16, CH), 0)
    extra = jnp.zeros((16, CH), F32)
    for k in range(3):
        extra = jnp.where(row == k, jnp.broadcast_to(pieces[k], (16, CH)), extra)
    result = jnp.concatenate([step, extra.astype(BF16)], axis=0)
    for k in range(PLANE):
        out_ref[k] = result


def transposed(value):
    return jnp.concatenate([value, jnp.zeros((128 - A, 128), F32)], axis=0).T


def final_kernel(ids, strength, far_ref, step_ref, onsite_ref, probe_ref, cheb_ref, side_ref, colz_ref, colw_ref):
    own, zl, zh = ids()
    colz_ref[...] = columns(far_ref[own])
    colw_ref[...] = columns(step_ref[own])
    mine = pl.ds(pl.multiple_of(zl * A, A), A)
    zi, wi = colz_ref[mine], colw_ref[mine]
    near = [jnp.broadcast_to(zi[:, VEC + k:VEC + k + 1], (A, CH)) for k in range(4)]
    left = []
    for c in range(3):
        lanes = slice(c * PR, (c + 1) * PR)
        zc, wc = 0.5 * zi[:, lanes], -0.5 * wi[:, lanes]
        left.append(jnp.concatenate([zc, wc, -zc], axis=1))
    left = jnp.concatenate(left, axis=0).astype(BF16)
    row = lax.broadcasted_iota(jnp.int32, (A, CH), 0)
    lane = lax.broadcasted_iota(jnp.int32, (A, CH), 1)

    def chunk(jc, carry):
        gx, gy, gz, image, energy = carry
        meta = far_ref[jc, VEC:ROWS, :].astype(F32)
        rx, ry, rz, q2, a, b = geometry(
            *near, meta[0:1], meta[1:2], meta[2:3], meta[3:4] * strength)
        same = row + (own * CH + zl * A) == lane + jc * CH
        xx, xy, xz, yy, yz, zz = tensor(rx, ry, rz, jnp.where(same, 0.0, a), b)
        z, w = far_ref[jc, 0:VEC, :], step_ref[jc, 0:VEC, :]
        kinds = ((xx, xy, xz), (xy, yy, yz), (xz, yz, zz))
        weight = []
        for d in range(3):
            rows = slice(d * PR, (d + 1) * PR)
            tile = jnp.concatenate(kinds[d], axis=0).astype(BF16)
            image = image + lax.dot_general(w[rows], tile, NT, preferred_element_type=F32)
            right = jnp.concatenate([z[rows], z[rows], w[rows]], axis=0)
            weight.append(jnp.dot(left, right, preferred_element_type=F32))

        def wt(c, d):
            return weight[d][c * A:(c + 1) * A]

        trace = wt(0, 0) + wt(1, 1) + wt(2, 2)
        sxy, sxz, syz = wt(0, 1) + wt(1, 0), wt(0, 2) + wt(2, 0), wt(1, 2) + wt(2, 1)
        ux = 2.0 * wt(0, 0) * rx + sxy * ry + sxz * rz
        uy = sxy * rx + 2.0 * wt(1, 1) * ry + syz * rz
        uz = sxz * rx + syz * ry + 2.0 * wt(2, 2) * rz
        radial = trace - 2.5 * q2 * (rx * ux + ry * uy + rz * uz)
        gx = gx + b * (ux + rx * radial)
        gy = gy + b * (uy + ry * radial)
        gz = gz + b * (uz + rz * radial)
        piece = step_ref[jc, VEC:ROWS, :].astype(F32)
        energy = energy + (piece[0:1] + piece[1:2] + piece[2:3])
        return gx, gy, gz, image, energy

    zero = jnp.zeros((A, CH), F32)
    gx, gy, gz, image, energy = lax.fori_loop(
        0, PLANE, chunk,
        (zero, zero, zero, jnp.zeros((PR, 3 * A), F32), jnp.zeros((1, CH), F32)))
    w_rows = transposed(wi)
    for c in range(3):
        both = image[:, c * A:(c + 1) * A]
        w_both = w_rows[c * PR:(c + 1) * PR, 0:A]
        high = jnp.full((NP, A), zh, jnp.int32) > 0
        part = jnp.where(high, both[NP:], both[:NP])
        w = jnp.where(high, w_both[NP:], w_both[:NP])
        cheb_ref[c] = 2.0 * (onsite_ref[...] * w + part) - probe_ref[c].astype(F32)
    out = []
    for g in (gx, gy, gz):
        out.append(jnp.sum(transposed(g[:, 0:128] + g[:, 128:256]), axis=0, keepdims=True))
    out.append(energy[:, 0:128])
    side = jnp.concatenate(out, axis=0)
    side_ref[...] = side


def spec():
    return pl.BlockSpec(memory_space=pltpu.VMEM)


def call(kernel, outs, scratch, operands):
    return pl.pallas_call(
        kernel,
        out_shape=outs,
        in_specs=[spec() for _ in operands],
        out_specs=jax.tree.map(lambda _: spec(), outs),
        scratch_shapes=scratch,
        compiler_params=pltpu.CompilerParams(vmem_limit_bytes=VMEM),
    )(*operands)


def pack(positions, scales, onsite, probes):
    return call(pack_kernel, jax.ShapeDtypeStruct((LINE, 16, 4 * A), BF16), [],
                (positions, scales, onsite, probes))


def line(gathered):
    return call(line_kernel, jax.ShapeDtypeStruct((PLANE, ROWS, CH), BF16), [], (gathered,))


def step(ids, strength, far):
    def kernel(*refs):
        step_kernel(ids, strength, *refs)
    scratch = [pltpu.VMEM((6, CH, CH), BF16), pltpu.VMEM((4, CH, 128), F32), pltpu.VMEM((VEC, CH), F32)]
    return call(kernel, jax.ShapeDtypeStruct((PLANE, ROWS, CH), BF16), scratch, (far,))


def final(ids, strength, far, steps, onsite, probes):
    def kernel(*refs):
        final_kernel(ids, strength, *refs)
    outs = (jax.ShapeDtypeStruct((3, NP, A), F32), jax.ShapeDtypeStruct((4, 128), F32))
    scratch = [pltpu.VMEM((CH, 128), F32), pltpu.VMEM((CH, 128), F32)]
    return call(kernel, outs, scratch, (far, steps, onsite, probes))


def place():
    return (lax.axis_index("x") * NY + lax.axis_index("y"), lax.axis_index("zl"), lax.axis_index("zh"))


def body(positions, scales, onsite, probes):
    atoms = A * NX * NZL * NY
    probe_total = NP * NZH * NC
    strength = 4.0 / math.sqrt(atoms)
    scales, onsite = scales[None, :], onsite[None, :]
    sent = pack(positions, scales, onsite, probes)
    gathered = lax.all_to_all(sent, ("zl", "zh"), 0, 0, tiled=True)
    far = lax.all_to_all(line(gathered), ("x", "y"), 0, 0, tiled=True)
    steps = lax.all_to_all(step(place, strength, far), ("x", "y"), 0, 0, tiled=True)
    cheb, side = final(place, strength, far, steps, onsite, probes)
    other = lax.ppermute(side, "c", [(0, 1), (1, 0)])
    both = side + other
    forces = (-2.0 / probe_total) * both[0:3, 0:A]
    energy = both[3, 0] / probe_total
    return cheb, forces, energy


def solution(mesh):
    fine = Mesh(mesh.devices.reshape(NX, NZL, NY, NZH, NC), ("x", "zl", "y", "zh", "c"))
    blk, probe = ("x", "zl", "y"), ("zh", "c")
    return jax.shard_map(
        body,
        mesh=fine,
        in_specs=(P(None, blk), P(blk), P(blk), P(None, probe, blk)),
        out_specs=(P(None, probe, blk), P(None, blk), P()),
        check_vma=False,
    )
```

```python
import math

import jax
import jax.numpy as jnp
from jax import lax
from jax.experimental import pallas as pl
from jax.experimental.pallas import tpu as pltpu
from jax.sharding import Mesh, PartitionSpec as P

SOFT_SQ = 0.25
F32 = jnp.float32
BF16 = jnp.bfloat16

NX, NZL, NY, NZH, NC = 4, 8, 4, 2, 2
PLANE = NX * NY
LINE = NZL * NZH
A = 32
NP = 16
CH = NZL * A
PR = NZH * NP
VEC = 3 * PR
ROWS = VEC + 16
VMEM = 48 * 1024 * 1024


def split3(value):
    hi = value.astype(BF16)
    rest = value - hi.astype(F32)
    mid = rest.astype(BF16)
    low = (rest - mid.astype(F32)).astype(BF16)
    return hi.astype(F32), mid.astype(F32), low.astype(F32)


def pack_kernel(pos_ref, scale_ref, onsite_ref, probe_ref, out_ref):
    hi, mid, low = split3(onsite_ref[...])
    row = lax.broadcasted_iota(jnp.int32, (16, A), 0)
    meta = jnp.zeros((16, A), F32)
    pos = pos_ref[...].astype(F32)
    values = [pos[0:1], pos[1:2], pos[2:3], scale_ref[...].astype(F32), hi, mid, low]
    for k, value in enumerate(values):
        meta = jnp.where(row == k, jnp.broadcast_to(value, (16, A)), meta)
    parts = [probe_ref[c].astype(F32) for c in range(3)] + [meta]
    packet = jnp.concatenate(parts, axis=1).astype(BF16)
    for k in range(LINE):
        out_ref[k] = packet


def line_kernel(in_ref, out_ref):
    parts = []
    for q in range(3):
        for zh in range(NZH):
            parts.append(jnp.concatenate(
                [in_ref[zl * NZH + zh, :, q * A:(q + 1) * A] for zl in range(NZL)], axis=1))
    parts.append(jnp.concatenate(
        [in_ref[zl * NZH, :, 3 * A:4 * A] for zl in range(NZL)], axis=1))
    packet = jnp.concatenate(parts, axis=0)
    for k in range(PLANE):
        out_ref[k] = packet


def geometry(xi, yi, zi, si, xj, yj, zj, sj):
    rx, ry, rz = xi - xj, yi - yj, zi - zj
    q = lax.rsqrt(rx * rx + ry * ry + rz * rz + SOFT_SQ)
    q2 = q * q
    a = (si * sj) * (q2 * q)
    b = (3.0 * a) * q2
    return rx, ry, rz, q2, a, b


def tensor(rx, ry, rz, a, b):
    tx, ty, tz = rx * b, ry * b, rz * b
    return (tx * rx - a, tx * ry, tx * rz, ty * ry - a, ty * rz, tz * rz - a)


NT = (((1,), (1,)), ((), ()))


def columns(packet):
    wide = jnp.concatenate([packet.astype(F32), jnp.zeros((128 - ROWS, CH), F32)], axis=0)
    return wide.T


def step_kernel(ids, strength, far_ref, out_ref, even_ref, odd_ref, col_ref, acc_ref):
    own = ids()[0]
    packet = far_ref[own]
    values = packet[VEC:ROWS].astype(F32)
    xi, yi, zi, si = (values[k:k + 1] for k in range(4))
    si = si * strength
    rows4 = [far_ref[jc, VEC:ROWS, :].astype(F32)[0:4] for jc in range(PLANE)]
    rows4.append(jnp.zeros((128 - 4 * PLANE, CH), F32))
    turned = jnp.concatenate(rows4, axis=0).T
    for jc in range(PLANE):
        for k in range(4):
            col_ref[jc, k] = jnp.broadcast_to(turned[:, 4 * jc + k:4 * jc + k + 1], (CH, 128))
    acc_ref[...] = jnp.zeros_like(acc_ref)
    sub = 16
    ahead = (lax.broadcasted_iota(jnp.int32, (sub, 128), 0)
             - lax.broadcasted_iota(jnp.int32, (sub, 128), 1))

    def build(jc, tile_ref):
        gap = (own - jc) * CH
        for j0 in range(0, CH, sub):
            rows = slice(j0, j0 + sub)
            far = [col_ref[jc, k, rows] for k in range(4)]
            for half in range(2):
                lanes = slice(half * 128, half * 128 + 128)
                rx, ry, rz, _, a, b = geometry(
                    *far, xi[:, lanes], yi[:, lanes], zi[:, lanes], si[:, lanes])
                if j0 // 128 == half:
                    a = jnp.where(ahead == gap + (half * 128 - j0), 0.0, a)
                for k, value in enumerate(tensor(rx, ry, rz, a, b)):
                    tile_ref[k, rows, lanes] = value.astype(BF16)

    def multiply(jc, tile_ref):
        vec = far_ref[jc, 0:VEC, :]
        vx, vy, vz = vec[0:PR], vec[PR:2 * PR], vec[2 * PR:]

        def times(lhs, k):
            return jnp.dot(lhs, tile_ref[k], preferred_element_type=F32)

        xx, yy, zz = times(vx, 0), times(vy, 3), times(vz, 5)
        xy = times(vec[0:2 * PR], 1)
        yz = times(vec[PR:], 4)
        xz = times(jnp.concatenate([vx, vz], axis=0), 2)
        acc_ref[0:PR] += xx + xy[PR:] + xz[PR:]
        acc_ref[PR:2 * PR] += yy + xy[:PR] + yz[PR:]
        acc_ref[2 * PR:] += zz + xz[:PR] + yz[:PR]

    build(0, even_ref)

    def turn(jc, carry):
        @pl.when(lax.rem(jc, 2) == 0)
        def _():
            build(jc + 1, odd_ref)
            multiply(jc, even_ref)

        @pl.when((lax.rem(jc, 2) == 1) & (jc < PLANE - 1))
        def _():
            build(jc + 1, even_ref)
            multiply(jc, odd_ref)
        return carry

    lax.fori_loop(0, PLANE, turn, 0)
    multiply(PLANE - 1, odd_ref)
    onsite = values[4:5] + values[5:6] + values[6:7]
    z = packet[0:VEC].astype(F32)
    exact = onsite * z + acc_ref[...]
    step = exact.astype(BF16)
    w = step.astype(F32)
    part = 0.5 * (z - exact) * w + 0.25 * z * z
    total = jnp.sum(jnp.sum(part, axis=0, keepdims=True), axis=1, keepdims=True)
    pieces = split3(total)
    row = lax.broadcasted_iota(jnp.int32, (16, CH), 0)
    extra = jnp.zeros((16, CH), F32)
    for k in range(3):
        extra = jnp.where(row == k, jnp.broadcast_to(pieces[k], (16, CH)), extra)
    result = jnp.concatenate([step, extra.astype(BF16)], axis=0)
    for k in range(PLANE):
        out_ref[k] = result


def transposed(value):
    return jnp.concatenate([value, jnp.zeros((128 - A, 128), F32)], axis=0).T


def final_kernel(ids, strength, far_ref, step_ref, onsite_ref, probe_ref, cheb_ref, side_ref, colz_ref, colw_ref):
    own, zl, zh = ids()
    colz_ref[...] = columns(far_ref[own])
    colw_ref[...] = columns(step_ref[own])
    mine = pl.ds(pl.multiple_of(zl * A, A), A)
    zi, wi = colz_ref[mine], colw_ref[mine]
    near = [jnp.broadcast_to(zi[:, VEC + k:VEC + k + 1], (A, CH)) for k in range(4)]
    left = []
    for c in range(3):
        lanes = slice(c * PR, (c + 1) * PR)
        zc, wc = 0.5 * zi[:, lanes], -0.5 * wi[:, lanes]
        left.append(jnp.concatenate([zc, wc, -zc], axis=1))
    left = jnp.concatenate(left, axis=0).astype(BF16)
    row = lax.broadcasted_iota(jnp.int32, (A, CH), 0)
    lane = lax.broadcasted_iota(jnp.int32, (A, CH), 1)

    def chunk(jc, carry):
        gx, gy, gz, image, energy = carry
        meta = far_ref[jc, VEC:ROWS, :].astype(F32)
        rx, ry, rz, q2, a, b = geometry(
            *near, meta[0:1], meta[1:2], meta[2:3], meta[3:4] * strength)
        same = row + (own * CH + zl * A) == lane + jc * CH
        xx, xy, xz, yy, yz, zz = tensor(rx, ry, rz, jnp.where(same, 0.0, a), b)
        z, w = far_ref[jc, 0:VEC, :], step_ref[jc, 0:VEC, :]
        kinds = ((xx, xy, xz), (xy, yy, yz), (xz, yz, zz))
        weight = []
        for d in range(3):
            rows = slice(d * PR, (d + 1) * PR)
            tile = jnp.concatenate(kinds[d], axis=0).astype(BF16)
            image = image + lax.dot_general(w[rows], tile, NT, preferred_element_type=F32)
            right = jnp.concatenate([z[rows], z[rows], w[rows]], axis=0)
            weight.append(jnp.dot(left, right, preferred_element_type=F32))

        def wt(c, d):
            return weight[d][c * A:(c + 1) * A]

        trace = wt(0, 0) + wt(1, 1) + wt(2, 2)
        sxy, sxz, syz = wt(0, 1) + wt(1, 0), wt(0, 2) + wt(2, 0), wt(1, 2) + wt(2, 1)
        ux = 2.0 * wt(0, 0) * rx + sxy * ry + sxz * rz
        uy = sxy * rx + 2.0 * wt(1, 1) * ry + syz * rz
        uz = sxz * rx + syz * ry + 2.0 * wt(2, 2) * rz
        radial = trace - 2.5 * q2 * (rx * ux + ry * uy + rz * uz)
        gx = gx + b * (ux + rx * radial)
        gy = gy + b * (uy + ry * radial)
        gz = gz + b * (uz + rz * radial)
        piece = step_ref[jc, VEC:ROWS, :].astype(F32)
        energy = energy + (piece[0:1] + piece[1:2] + piece[2:3])
        return gx, gy, gz, image, energy

    zero = jnp.zeros((A, CH), F32)
    gx, gy, gz, image, energy = lax.fori_loop(
        0, PLANE, chunk,
        (zero, zero, zero, jnp.zeros((PR, 3 * A), F32), jnp.zeros((1, CH), F32)),
        unroll=8)
    w_rows = transposed(wi)
    for c in range(3):
        both = image[:, c * A:(c + 1) * A]
        w_both = w_rows[c * PR:(c + 1) * PR, 0:A]
        high = jnp.full((NP, A), zh, jnp.int32) > 0
        part = jnp.where(high, both[NP:], both[:NP])
        w = jnp.where(high, w_both[NP:], w_both[:NP])
        cheb_ref[c] = 2.0 * (onsite_ref[...] * w + part) - probe_ref[c].astype(F32)
    out = []
    for g in (gx, gy, gz):
        out.append(jnp.sum(transposed(g[:, 0:128] + g[:, 128:256]), axis=0, keepdims=True))
    out.append(energy[:, 0:128])
    side = jnp.concatenate(out, axis=0)
    side_ref[...] = side


def spec():
    return pl.BlockSpec(memory_space=pltpu.VMEM)


def call(kernel, outs, scratch, operands):
    return pl.pallas_call(
        kernel,
        out_shape=outs,
        in_specs=[spec() for _ in operands],
        out_specs=jax.tree.map(lambda _: spec(), outs),
        scratch_shapes=scratch,
        compiler_params=pltpu.CompilerParams(vmem_limit_bytes=VMEM),
    )(*operands)


def pack(positions, scales, onsite, probes):
    return call(pack_kernel, jax.ShapeDtypeStruct((LINE, 16, 4 * A), BF16), [],
                (positions, scales, onsite, probes))


def line(gathered):
    return call(line_kernel, jax.ShapeDtypeStruct((PLANE, ROWS, CH), BF16), [], (gathered,))


def step(ids, strength, far):
    def kernel(*refs):
        step_kernel(ids, strength, *refs)
    scratch = [pltpu.VMEM((6, CH, CH), BF16), pltpu.VMEM((6, CH, CH), BF16), pltpu.VMEM((PLANE, 4, CH, 128), F32), pltpu.VMEM((VEC, CH), F32)]
    return call(kernel, jax.ShapeDtypeStruct((PLANE, ROWS, CH), BF16), scratch, (far,))


def final(ids, strength, far, steps, onsite, probes):
    def kernel(*refs):
        final_kernel(ids, strength, *refs)
    outs = (jax.ShapeDtypeStruct((3, NP, A), F32), jax.ShapeDtypeStruct((4, 128), F32))
    scratch = [pltpu.VMEM((CH, 128), F32), pltpu.VMEM((CH, 128), F32)]
    return call(kernel, outs, scratch, (far, steps, onsite, probes))


def end_kernel(probe_total, side_ref, other_ref, forces_ref, energy_ref):
    both = side_ref[...] + other_ref[...]
    forces_ref[...] = (-2.0 / probe_total) * both[0:3, 0:A]
    energy_ref[...] = both[3:4, 0:1] / probe_total


def end(probe_total, side, other):
    def kernel(*refs):
        end_kernel(probe_total, *refs)
    outs = (jax.ShapeDtypeStruct((3, A), F32), jax.ShapeDtypeStruct((1, 1), F32))
    return call(kernel, outs, [], (side, other))


def place():
    return (lax.axis_index("x") * NY + lax.axis_index("y"), lax.axis_index("zl"), lax.axis_index("zh"))


def body(positions, scales, onsite, probes):
    atoms = A * NX * NZL * NY
    probe_total = NP * NZH * NC
    strength = 4.0 / math.sqrt(atoms)
    scales, onsite = scales[None, :], onsite[None, :]
    sent = pack(positions, scales, onsite, probes)
    gathered = lax.all_to_all(sent, ("zl", "zh"), 0, 0, tiled=True)
    far = lax.all_to_all(line(gathered), ("x", "y"), 0, 0, tiled=True)
    steps = lax.all_to_all(step(place, strength, far), ("x", "y"), 0, 0, tiled=True)
    cheb, side = final(place, strength, far, steps, onsite, probes)
    other = lax.ppermute(side, "c", [(0, 1), (1, 0)])
    forces, energy = end(probe_total, side, other)
    return cheb, forces, energy.reshape(())


def solution(mesh):
    fine = Mesh(mesh.devices.reshape(NX, NZL, NY, NZH, NC), ("x", "zl", "y", "zh", "c"))
    blk, probe = ("x", "zl", "y"), ("zh", "c")
    return jax.shard_map(
        body,
        mesh=fine,
        in_specs=(P(None, blk), P(blk), P(blk), P(None, probe, blk)),
        out_specs=(P(None, probe, blk), P(None, blk), P()),
        check_vma=False,
    )
```

```python
import math

import jax
import jax.numpy as jnp
from jax import lax
from jax.experimental import pallas as pl
from jax.experimental.pallas import tpu as pltpu
from jax.sharding import Mesh, PartitionSpec as P

SOFT_SQ = 0.25
F32 = jnp.float32
BF16 = jnp.bfloat16

NX, NZL, NY, NZH, NC = 4, 8, 4, 2, 2
PLANE = NX * NY
LINE = NZL * NZH
A = 32
NP = 16
CH = NZL * A
PR = NZH * NP
VEC = 3 * PR
ROWS = 2 * VEC + 16
HALF = CH // 2
VMEM = 48 * 1024 * 1024


def split3(value):
    hi = value.astype(BF16)
    rest = value - hi.astype(F32)
    mid = rest.astype(BF16)
    low = (rest - mid.astype(F32)).astype(BF16)
    return hi.astype(F32), mid.astype(F32), low.astype(F32)


def pack_kernel(pos_in, scale_in, onsite_in, probe_in, out_ref, pos_ref, scale_ref, onsite_ref, probe_ref, sems):
    pairs = ((pos_in, pos_ref), (scale_in, scale_ref), (onsite_in, onsite_ref), (probe_in, probe_ref))
    copies = [pltpu.make_async_copy(a, b, sems.at[k]) for k, (a, b) in enumerate(pairs)]
    for copy in copies:
        copy.start()
    for copy in copies:
        copy.wait()
    hi, mid, low = split3(onsite_ref[...])
    row = lax.broadcasted_iota(jnp.int32, (16, A), 0)
    meta = jnp.zeros((16, A), F32)
    pos = pos_ref[...].astype(F32)
    values = [pos[0:1], pos[1:2], pos[2:3], scale_ref[...].astype(F32), hi, mid, low]
    for k, value in enumerate(values):
        meta = jnp.where(row == k, jnp.broadcast_to(value, (16, A)), meta)
    parts = [probe_ref[c].astype(F32) for c in range(3)] + [meta]
    packet = jnp.concatenate(parts, axis=1).astype(BF16)
    for k in range(LINE):
        out_ref[k] = packet


def line_kernel(in_ref, out_ref):
    parts, values = [], []
    for first in (0, NZL // 2):
        lines = range(first, first + NZL // 2)
        for q in range(3):
            for zh in range(NZH):
                parts.append(jnp.concatenate(
                    [in_ref[zl * NZH + zh, :, q * A:(q + 1) * A] for zl in lines], axis=1))
        values.append(jnp.concatenate(
            [in_ref[zl * NZH, :, 3 * A:4 * A].astype(F32) for zl in lines], axis=1)[0:8])
    parts.append(jnp.concatenate(values, axis=0).astype(BF16))
    packet = jnp.concatenate(parts, axis=0)
    for k in range(PLANE):
        out_ref[k] = packet


def vectors_of(ref, k):
    return jnp.concatenate([ref[k, 0:VEC], ref[k, VEC:2 * VEC]], axis=1)


def values_of(ref, k):
    both = ref[k, 2 * VEC:ROWS].astype(F32)
    return jnp.concatenate([both[0:8], both[8:16]], axis=1)


def geometry(xi, yi, zi, si, xj, yj, zj, sj):
    rx, ry, rz = xi - xj, yi - yj, zi - zj
    q = lax.rsqrt(rx * rx + ry * ry + rz * rz + SOFT_SQ)
    q2 = q * q
    a = (si * sj) * (q2 * q)
    b = (3.0 * a) * q2
    return rx, ry, rz, q2, a, b


def tensor(rx, ry, rz, a, b):
    tx, ty, tz = rx * b, ry * b, rz * b
    return (tx * rx - a, tx * ry, tx * rz, ty * ry - a, ty * rz, tz * rz - a)


NT = (((1,), (1,)), ((), ()))


def columns(vectors, values):
    rest = jnp.zeros((128 - VEC - values.shape[0], CH), F32)
    return jnp.concatenate([vectors.astype(F32), values, rest], axis=0).T


def step_kernel(ids, strength, far_ref, out_ref, even_ref, odd_ref, col_ref, acc_ref):
    own = ids()[0]
    values = values_of(far_ref, own)
    xi, yi, zi, si = (values[k:k + 1] for k in range(4))
    si = si * strength
    rows4 = [values_of(far_ref, jc)[0:4] for jc in range(PLANE)]
    rows4.append(jnp.zeros((128 - 4 * PLANE, CH), F32))
    turned = jnp.concatenate(rows4, axis=0).T
    for jc in range(PLANE):
        for k in range(4):
            col_ref[jc, k] = jnp.broadcast_to(turned[:, 4 * jc + k:4 * jc + k + 1], (CH, 128))
    acc_ref[...] = jnp.zeros_like(acc_ref)
    sub = 16
    ahead = (lax.broadcasted_iota(jnp.int32, (sub, 128), 0)
             - lax.broadcasted_iota(jnp.int32, (sub, 128), 1))

    def build(jc, tile_ref):
        gap = (own - jc) * CH
        for j0 in range(0, CH, sub):
            rows = slice(j0, j0 + sub)
            far = [col_ref[jc, k, rows] for k in range(4)]
            for half in range(2):
                lanes = slice(half * 128, half * 128 + 128)
                rx, ry, rz, _, a, b = geometry(
                    *far, xi[:, lanes], yi[:, lanes], zi[:, lanes], si[:, lanes])
                if j0 // 128 == half:
                    a = jnp.where(ahead == gap + (half * 128 - j0), 0.0, a)
                for k, value in enumerate(tensor(rx, ry, rz, a, b)):
                    tile_ref[k, rows, lanes] = value.astype(BF16)

    def multiply(jc, tile_ref):
        vec = vectors_of(far_ref, jc)
        vx, vy, vz = vec[0:PR], vec[PR:2 * PR], vec[2 * PR:]

        def times(lhs, k):
            return jnp.dot(lhs, tile_ref[k], preferred_element_type=F32)

        xx, yy, zz = times(vx, 0), times(vy, 3), times(vz, 5)
        xy = times(vec[0:2 * PR], 1)
        yz = times(vec[PR:], 4)
        xz = times(jnp.concatenate([vx, vz], axis=0), 2)
        acc_ref[0:PR] += xx + xy[PR:] + xz[PR:]
        acc_ref[PR:2 * PR] += yy + xy[:PR] + yz[PR:]
        acc_ref[2 * PR:] += zz + xz[:PR] + yz[:PR]

    build(0, even_ref)

    def turn(jc, carry):
        @pl.when(lax.rem(jc, 2) == 0)
        def _():
            build(jc + 1, odd_ref)
            multiply(jc, even_ref)

        @pl.when((lax.rem(jc, 2) == 1) & (jc < PLANE - 1))
        def _():
            build(jc + 1, even_ref)
            multiply(jc, odd_ref)
        return carry

    lax.fori_loop(0, PLANE, turn, 0)
    multiply(PLANE - 1, odd_ref)
    onsite = values[4:5] + values[5:6] + values[6:7]
    z = vectors_of(far_ref, own).astype(F32)
    exact = onsite * z + acc_ref[...]
    step = exact.astype(BF16)
    w = step.astype(F32)
    part = 0.5 * (z - exact) * w + 0.25 * z * z
    total = jnp.sum(jnp.sum(part, axis=0, keepdims=True), axis=1, keepdims=True)
    pieces = split3(total)
    row = lax.broadcasted_iota(jnp.int32, (16, HALF), 0)
    extra = jnp.zeros((16, HALF), F32)
    for k in range(3):
        extra = jnp.where(row == k, jnp.broadcast_to(pieces[k], (16, HALF)), extra)
    result = jnp.concatenate([step[:, :HALF], step[:, HALF:], extra.astype(BF16)], axis=0)
    for k in range(PLANE):
        out_ref[k] = result


def transposed(value):
    return jnp.concatenate([value, jnp.zeros((128 - A, 128), F32)], axis=0).T


def final_kernel(ids, strength, far_ref, step_ref, onsite_ref, probe_ref, cheb_ref, side_ref, colz_ref, colw_ref):
    own, zl, zh = ids()
    colz_ref[...] = columns(vectors_of(far_ref, own), values_of(far_ref, own))
    colw_ref[...] = columns(vectors_of(step_ref, own), jnp.zeros((8, CH), F32))
    mine = pl.ds(pl.multiple_of(zl * A, A), A)
    zi, wi = colz_ref[mine], colw_ref[mine]
    near = [jnp.broadcast_to(zi[:, VEC + k:VEC + k + 1], (A, CH)) for k in range(4)]
    left = []
    for c in range(3):
        lanes = slice(c * PR, (c + 1) * PR)
        zc, wc = 0.5 * zi[:, lanes], -0.5 * wi[:, lanes]
        left.append(jnp.concatenate([zc, wc, -zc], axis=1))
    left = jnp.concatenate(left, axis=0).astype(BF16)
    row = lax.broadcasted_iota(jnp.int32, (A, CH), 0)
    lane = lax.broadcasted_iota(jnp.int32, (A, CH), 1)

    def chunk(jc, carry):
        gx, gy, gz, image, energy = carry
        meta = values_of(far_ref, jc)
        rx, ry, rz, q2, a, b = geometry(
            *near, meta[0:1], meta[1:2], meta[2:3], meta[3:4] * strength)
        same = row + (own * CH + zl * A) == lane + jc * CH
        xx, xy, xz, yy, yz, zz = tensor(rx, ry, rz, jnp.where(same, 0.0, a), b)
        z, w = vectors_of(far_ref, jc), vectors_of(step_ref, jc)
        kinds = ((xx, xy, xz), (xy, yy, yz), (xz, yz, zz))
        weight = []
        for d in range(3):
            rows = slice(d * PR, (d + 1) * PR)
            tile = jnp.concatenate(kinds[d], axis=0).astype(BF16)
            image = image + lax.dot_general(w[rows], tile, NT, preferred_element_type=F32)
            right = jnp.concatenate([z[rows], z[rows], w[rows]], axis=0)
            weight.append(jnp.dot(left, right, preferred_element_type=F32))

        def wt(c, d):
            return weight[d][c * A:(c + 1) * A]

        trace = wt(0, 0) + wt(1, 1) + wt(2, 2)
        sxy, sxz, syz = wt(0, 1) + wt(1, 0), wt(0, 2) + wt(2, 0), wt(1, 2) + wt(2, 1)
        ux = 2.0 * wt(0, 0) * rx + sxy * ry + sxz * rz
        uy = sxy * rx + 2.0 * wt(1, 1) * ry + syz * rz
        uz = sxz * rx + syz * ry + 2.0 * wt(2, 2) * rz
        radial = trace - 2.5 * q2 * (rx * ux + ry * uy + rz * uz)
        gx = gx + b * (ux + rx * radial)
        gy = gy + b * (uy + ry * radial)
        gz = gz + b * (uz + rz * radial)
        piece = step_ref[jc, 2 * VEC:ROWS].astype(F32)
        energy = energy + (piece[0:1] + piece[1:2] + piece[2:3])
        return gx, gy, gz, image, energy

    zero = jnp.zeros((A, CH), F32)
    gx, gy, gz, image, energy = lax.fori_loop(
        0, PLANE, chunk,
        (zero, zero, zero, jnp.zeros((PR, 3 * A), F32), jnp.zeros((1, HALF), F32)),
        unroll=8)
    w_rows = transposed(wi)
    for c in range(3):
        both = image[:, c * A:(c + 1) * A]
        w_both = w_rows[c * PR:(c + 1) * PR, 0:A]
        high = jnp.full((NP, A), zh, jnp.int32) > 0
        part = jnp.where(high, both[NP:], both[:NP])
        w = jnp.where(high, w_both[NP:], w_both[:NP])
        cheb_ref[c] = 2.0 * (onsite_ref[...] * w + part) - probe_ref[c].astype(F32)
    out = []
    for g in (gx, gy, gz):
        out.append(jnp.sum(transposed(g[:, 0:128] + g[:, 128:256]), axis=0, keepdims=True))
    out.append(energy)
    side = jnp.concatenate(out, axis=0)
    side_ref[...] = side


def spec():
    return pl.BlockSpec(memory_space=pltpu.VMEM)


def call(kernel, outs, scratch, operands):
    return pl.pallas_call(
        kernel,
        out_shape=outs,
        in_specs=[spec() for _ in operands],
        out_specs=jax.tree.map(lambda _: spec(), outs),
        scratch_shapes=scratch,
        compiler_params=pltpu.CompilerParams(vmem_limit_bytes=VMEM),
    )(*operands)


def pack(*operands):
    scratch = [pltpu.VMEM(x.shape, x.dtype) for x in operands] + [pltpu.SemaphoreType.DMA((4,))]
    return pl.pallas_call(
        pack_kernel,
        out_shape=jax.ShapeDtypeStruct((LINE, 16, 4 * A), BF16),
        in_specs=[pl.BlockSpec(memory_space=pltpu.HBM) for _ in operands],
        out_specs=spec(),
        scratch_shapes=scratch,
        compiler_params=pltpu.CompilerParams(vmem_limit_bytes=VMEM),
    )(*(pltpu.with_memory_space_constraint(x, pltpu.HBM) for x in operands))


def line(gathered):
    return call(line_kernel, jax.ShapeDtypeStruct((PLANE, ROWS, HALF), BF16), [], (gathered,))


def step(ids, strength, far):
    def kernel(*refs):
        step_kernel(ids, strength, *refs)
    scratch = [pltpu.VMEM((6, CH, CH), BF16), pltpu.VMEM((6, CH, CH), BF16), pltpu.VMEM((PLANE, 4, CH, 128), F32), pltpu.VMEM((VEC, CH), F32)]
    return call(kernel, jax.ShapeDtypeStruct((PLANE, ROWS, HALF), BF16), scratch, (far,))


def final(ids, strength, far, steps, onsite, probes):
    def kernel(*refs):
        final_kernel(ids, strength, *refs)
    outs = (jax.ShapeDtypeStruct((3, NP, A), F32), jax.ShapeDtypeStruct((4, 128), F32))
    scratch = [pltpu.VMEM((CH, 128), F32), pltpu.VMEM((CH, 128), F32)]
    return call(kernel, outs, scratch, (far, steps, onsite, probes))


def end_kernel(probe_total, side_ref, other_ref, forces_ref, energy_ref):
    both = side_ref[...] + other_ref[...]
    forces_ref[...] = (-2.0 / probe_total) * both[0:3, 0:A]
    energy_ref[...] = both[3:4, 0:1] / probe_total


def end(probe_total, side, other):
    def kernel(*refs):
        end_kernel(probe_total, *refs)
    outs = (jax.ShapeDtypeStruct((3, A), F32), jax.ShapeDtypeStruct((1, 1), F32))
    return call(kernel, outs, [], (side, other))


def place():
    return (lax.axis_index("x") * NY + lax.axis_index("y"), lax.axis_index("zl"), lax.axis_index("zh"))


def body(positions, scales, onsite, probes):
    atoms = A * NX * NZL * NY
    probe_total = NP * NZH * NC
    strength = 4.0 / math.sqrt(atoms)
    scales, onsite = scales[None, :], onsite[None, :]
    sent = pack(positions, scales, onsite, probes)
    gathered = lax.all_to_all(sent, ("zl", "zh"), 0, 0, tiled=True)
    far = lax.all_to_all(line(gathered), ("x", "y"), 0, 0, tiled=True)
    steps = lax.all_to_all(step(place, strength, far), ("x", "y"), 0, 0, tiled=True)
    cheb, side = final(place, strength, far, steps, onsite, probes)
    other = lax.ppermute(side, "c", [(0, 1), (1, 0)])
    forces, energy = end(probe_total, side, other)
    return cheb, forces, energy.reshape(())


def solution(mesh):
    fine = Mesh(mesh.devices.reshape(NX, NZL, NY, NZH, NC), ("x", "zl", "y", "zh", "c"))
    blk, probe = ("x", "zl", "y"), ("zh", "c")
    return jax.shard_map(
        body,
        mesh=fine,
        in_specs=(P(None, blk), P(blk), P(blk), P(None, probe, blk)),
        out_specs=(P(None, probe, blk), P(None, blk), P()),
        check_vma=False,
    )
```

```python
import math

import jax
import jax.numpy as jnp
from jax import lax
from jax.experimental import pallas as pl
from jax.experimental.pallas import tpu as pltpu
from jax.sharding import Mesh, PartitionSpec as P

SOFT_SQ = 0.25
F32 = jnp.float32
BF16 = jnp.bfloat16

NX, NZL, NY, NZH, NC = 4, 8, 4, 2, 2
PLANE = NX * NY
LINE = NZL * NZH
A = 32
NP = 16
CH = NZL * A
PR = NZH * NP
VEC = 3 * PR
ROWS = 2 * VEC + 16
HALF = CH // 2
VMEM = 48 * 1024 * 1024


def split3(value):
    hi = value.astype(BF16)
    rest = value - hi.astype(F32)
    mid = rest.astype(BF16)
    low = (rest - mid.astype(F32)).astype(BF16)
    return hi.astype(F32), mid.astype(F32), low.astype(F32)


def pack_kernel(pos_in, scale_in, onsite_in, probe_in, out_ref, pos_ref, scale_ref, onsite_ref, probe_ref, sems):
    pairs = ((pos_in, pos_ref), (scale_in, scale_ref), (onsite_in, onsite_ref), (probe_in, probe_ref))
    copies = [pltpu.make_async_copy(a, b, sems.at[k]) for k, (a, b) in enumerate(pairs)]
    for copy in copies:
        copy.start()
    for copy in copies:
        copy.wait()
    hi, mid, low = split3(onsite_ref[...])
    row = lax.broadcasted_iota(jnp.int32, (16, A), 0)
    meta = jnp.zeros((16, A), F32)
    pos = pos_ref[...].astype(F32)
    values = [pos[0:1], pos[1:2], pos[2:3], scale_ref[...].astype(F32), hi, mid, low]
    for k, value in enumerate(values):
        meta = jnp.where(row == k, jnp.broadcast_to(value, (16, A)), meta)
    parts = [probe_ref[c].astype(F32) for c in range(3)] + [meta]
    packet = jnp.concatenate(parts, axis=1).astype(BF16)
    for k in range(LINE):
        out_ref[k] = packet


def line_kernel(in_ref, out_ref):
    parts, values = [], []
    for first in (0, NZL // 2):
        lines = range(first, first + NZL // 2)
        for q in range(3):
            for zh in range(NZH):
                parts.append(jnp.concatenate(
                    [in_ref[zl * NZH + zh, :, q * A:(q + 1) * A] for zl in lines], axis=1))
        values.append(jnp.concatenate(
            [in_ref[zl * NZH, :, 3 * A:4 * A].astype(F32) for zl in lines], axis=1)[0:8])
    parts.append(jnp.concatenate(values, axis=0).astype(BF16))
    packet = jnp.concatenate(parts, axis=0)
    for k in range(PLANE):
        out_ref[k] = packet


def vectors_of(ref, k):
    return jnp.concatenate([ref[k, 0:VEC], ref[k, VEC:2 * VEC]], axis=1)


def values_of(ref, k):
    both = ref[k, 2 * VEC:ROWS].astype(F32)
    return jnp.concatenate([both[0:8], both[8:16]], axis=1)


def geometry(xi, yi, zi, si, xj, yj, zj, sj):
    rx, ry, rz = xi - xj, yi - yj, zi - zj
    q = lax.rsqrt(rx * rx + ry * ry + rz * rz + SOFT_SQ)
    q2 = q * q
    a = (si * sj) * (q2 * q)
    b = (3.0 * a) * q2
    return rx, ry, rz, q2, a, b


def tensor(rx, ry, rz, a, b):
    tx, ty, tz = rx * b, ry * b, rz * b
    return (tx * rx - a, tx * ry, tx * rz, ty * ry - a, ty * rz, tz * rz - a)


NT = (((1,), (1,)), ((), ()))


def columns(vectors, values):
    rest = jnp.zeros((128 - VEC - values.shape[0], CH), F32)
    return jnp.concatenate([vectors.astype(F32), values, rest], axis=0).T


def step_kernel(ids, strength, far_ref, out_ref, even_ref, odd_ref, col_ref, acc_ref):
    own = ids()[0]
    values = values_of(far_ref, own)
    turned = columns(vectors_of(far_ref, own), values)
    for k in range(4):
        col_ref[k] = jnp.broadcast_to(turned[:, VEC + k:VEC + k + 1], (CH, 128))
    acc_ref[...] = jnp.zeros_like(acc_ref)
    sub = 16
    ahead = (lax.broadcasted_iota(jnp.int32, (sub, 128), 0)
             - lax.broadcasted_iota(jnp.int32, (sub, 128), 1))

    def build(jc, tile_ref):
        gap = (jc - own) * CH
        v = values_of(far_ref, jc)
        xj, yj, zj, sj = v[0:1], v[1:2], v[2:3], v[3:4] * strength
        for i0 in range(0, CH, sub):
            rows = slice(i0, i0 + sub)
            near = [col_ref[k, rows] for k in range(4)]
            for half in range(2):
                lanes = slice(half * 128, half * 128 + 128)
                rx, ry, rz, _, a, b = geometry(
                    *near, xj[:, lanes], yj[:, lanes], zj[:, lanes], sj[:, lanes])
                if i0 // 128 == half:
                    a = jnp.where(ahead == gap + (half * 128 - i0), 0.0, a)
                for k, value in enumerate(tensor(rx, ry, rz, a, b)):
                    tile_ref[k, rows, lanes] = value.astype(BF16)

    def multiply(jc, tile_ref):
        vec = vectors_of(far_ref, jc)
        vx, vy, vz = vec[0:PR], vec[PR:2 * PR], vec[2 * PR:]

        def times(lhs, k):
            return lax.dot_general(lhs, tile_ref[k], NT, preferred_element_type=F32)

        xx, yy, zz = times(vx, 0), times(vy, 3), times(vz, 5)
        xy = times(vec[0:2 * PR], 1)
        yz = times(vec[PR:], 4)
        xz = times(jnp.concatenate([vx, vz], axis=0), 2)
        acc_ref[0:PR] += xx + xy[PR:] + xz[PR:]
        acc_ref[PR:2 * PR] += yy + xy[:PR] + yz[PR:]
        acc_ref[2 * PR:] += zz + xz[:PR] + yz[:PR]

    build(0, even_ref)

    def turn(jc, carry):
        @pl.when(lax.rem(jc, 2) == 0)
        def _():
            build(jc + 1, odd_ref)
            multiply(jc, even_ref)

        @pl.when((lax.rem(jc, 2) == 1) & (jc < PLANE - 1))
        def _():
            build(jc + 1, even_ref)
            multiply(jc, odd_ref)
        return carry

    lax.fori_loop(0, PLANE, turn, 0)
    multiply(PLANE - 1, odd_ref)
    onsite = values[4:5] + values[5:6] + values[6:7]
    z = vectors_of(far_ref, own).astype(F32)
    exact = onsite * z + acc_ref[...]
    step = exact.astype(BF16)
    w = step.astype(F32)
    part = 0.5 * (z - exact) * w + 0.25 * z * z
    total = jnp.sum(jnp.sum(part, axis=0, keepdims=True), axis=1, keepdims=True)
    pieces = split3(total)
    row = lax.broadcasted_iota(jnp.int32, (16, HALF), 0)
    extra = jnp.zeros((16, HALF), F32)
    for k in range(3):
        extra = jnp.where(row == k, jnp.broadcast_to(pieces[k], (16, HALF)), extra)
    result = jnp.concatenate([step[:, :HALF], step[:, HALF:], extra.astype(BF16)], axis=0)
    for k in range(PLANE):
        out_ref[k] = result


def transposed(value):
    return jnp.concatenate([value, jnp.zeros((128 - A, 128), F32)], axis=0).T


def final_kernel(ids, strength, far_ref, step_ref, onsite_ref, probe_ref, cheb_ref, side_ref, colz_ref, colw_ref):
    own, zl, zh = ids()
    colz_ref[...] = columns(vectors_of(far_ref, own), values_of(far_ref, own))
    colw_ref[...] = columns(vectors_of(step_ref, own), jnp.zeros((8, CH), F32))
    mine = pl.ds(pl.multiple_of(zl * A, A), A)
    zi, wi = colz_ref[mine], colw_ref[mine]
    near = [jnp.broadcast_to(zi[:, VEC + k:VEC + k + 1], (A, CH)) for k in range(4)]
    left = []
    for c in range(3):
        lanes = slice(c * PR, (c + 1) * PR)
        zc, wc = 0.5 * zi[:, lanes], -0.5 * wi[:, lanes]
        left.append(jnp.concatenate([zc, wc, -zc], axis=1))
    left = jnp.concatenate(left, axis=0).astype(BF16)
    row = lax.broadcasted_iota(jnp.int32, (A, CH), 0)
    lane = lax.broadcasted_iota(jnp.int32, (A, CH), 1)

    def chunk(jc, carry):
        gx, gy, gz, image, energy = carry
        meta = values_of(far_ref, jc)
        rx, ry, rz, q2, a, b = geometry(
            *near, meta[0:1], meta[1:2], meta[2:3], meta[3:4] * strength)
        same = row + (own * CH + zl * A) == lane + jc * CH
        xx, xy, xz, yy, yz, zz = tensor(rx, ry, rz, jnp.where(same, 0.0, a), b)
        z, w = vectors_of(far_ref, jc), vectors_of(step_ref, jc)
        kinds = ((xx, xy, xz), (xy, yy, yz), (xz, yz, zz))
        weight = []
        for d in range(3):
            rows = slice(d * PR, (d + 1) * PR)
            tile = jnp.concatenate(kinds[d], axis=0).astype(BF16)
            image = image + lax.dot_general(w[rows], tile, NT, preferred_element_type=F32)
            right = jnp.concatenate([z[rows], z[rows], w[rows]], axis=0)
            weight.append(jnp.dot(left, right, preferred_element_type=F32))

        def wt(c, d):
            return weight[d][c * A:(c + 1) * A]

        trace = wt(0, 0) + wt(1, 1) + wt(2, 2)
        sxy, sxz, syz = wt(0, 1) + wt(1, 0), wt(0, 2) + wt(2, 0), wt(1, 2) + wt(2, 1)
        ux = 2.0 * wt(0, 0) * rx + sxy * ry + sxz * rz
        uy = sxy * rx + 2.0 * wt(1, 1) * ry + syz * rz
        uz = sxz * rx + syz * ry + 2.0 * wt(2, 2) * rz
        radial = trace - 2.5 * q2 * (rx * ux + ry * uy + rz * uz)
        gx = gx + b * (ux + rx * radial)
        gy = gy + b * (uy + ry * radial)
        gz = gz + b * (uz + rz * radial)
        piece = step_ref[jc, 2 * VEC:ROWS].astype(F32)
        energy = energy + (piece[0:1] + piece[1:2] + piece[2:3])
        return gx, gy, gz, image, energy

    zero = jnp.zeros((A, CH), F32)
    gx, gy, gz, image, energy = lax.fori_loop(
        0, PLANE, chunk,
        (zero, zero, zero, jnp.zeros((PR, 3 * A), F32), jnp.zeros((1, HALF), F32)),
        unroll=16)
    w_rows = transposed(wi)
    for c in range(3):
        both = image[:, c * A:(c + 1) * A]
        w_both = w_rows[c * PR:(c + 1) * PR, 0:A]
        high = jnp.full((NP, A), zh, jnp.int32) > 0
        part = jnp.where(high, both[NP:], both[:NP])
        w = jnp.where(high, w_both[NP:], w_both[:NP])
        cheb_ref[c] = 2.0 * (onsite_ref[...] * w + part) - probe_ref[c].astype(F32)
    out = []
    for g in (gx, gy, gz):
        out.append(jnp.sum(transposed(g[:, 0:128] + g[:, 128:256]), axis=0, keepdims=True))
    out.append(energy)
    side = jnp.concatenate(out + [jnp.zeros((4, 128), F32)], axis=0)
    side_ref[...] = side


def spec():
    return pl.BlockSpec(memory_space=pltpu.VMEM)


def call(kernel, outs, scratch, operands):
    return pl.pallas_call(
        kernel,
        out_shape=outs,
        in_specs=[spec() for _ in operands],
        out_specs=jax.tree.map(lambda _: spec(), outs),
        scratch_shapes=scratch,
        compiler_params=pltpu.CompilerParams(vmem_limit_bytes=VMEM),
    )(*operands)


def pack(*operands):
    scratch = [pltpu.VMEM(x.shape, x.dtype) for x in operands] + [pltpu.SemaphoreType.DMA((4,))]
    return pl.pallas_call(
        pack_kernel,
        out_shape=jax.ShapeDtypeStruct((LINE, 16, 4 * A), BF16),
        in_specs=[pl.BlockSpec(memory_space=pltpu.HBM) for _ in operands],
        out_specs=spec(),
        scratch_shapes=scratch,
        compiler_params=pltpu.CompilerParams(vmem_limit_bytes=VMEM),
    )(*(pltpu.with_memory_space_constraint(x, pltpu.HBM) for x in operands))


def line(gathered):
    return call(line_kernel, jax.ShapeDtypeStruct((PLANE, ROWS, HALF), BF16), [], (gathered,))


def step(ids, strength, far):
    def kernel(*refs):
        step_kernel(ids, strength, *refs)
    scratch = [pltpu.VMEM((6, CH, CH), BF16), pltpu.VMEM((6, CH, CH), BF16), pltpu.VMEM((4, CH, 128), F32), pltpu.VMEM((VEC, CH), F32)]
    return call(kernel, jax.ShapeDtypeStruct((PLANE, ROWS, HALF), BF16), scratch, (far,))


def final(ids, strength, far, steps, onsite, probes):
    def kernel(*refs):
        final_kernel(ids, strength, *refs)
    outs = (jax.ShapeDtypeStruct((3, NP, A), F32), jax.ShapeDtypeStruct((8, 128), F32))
    scratch = [pltpu.VMEM((CH, 128), F32), pltpu.VMEM((CH, 128), F32)]
    return call(kernel, outs, scratch, (far, steps, onsite, probes))


def end_kernel(probe_total, side_ref, forces_ref, energy_ref):
    both = side_ref[0:8] + side_ref[8:16]
    forces_ref[...] = (-2.0 / probe_total) * both[0:3, 0:A]
    energy_ref[...] = both[3:4, 0:1] / probe_total


def end(probe_total, sides):
    def kernel(*refs):
        end_kernel(probe_total, *refs)
    outs = (jax.ShapeDtypeStruct((3, A), F32), jax.ShapeDtypeStruct((1, 1), F32))
    return call(kernel, outs, [], (sides,))


def place():
    return (lax.axis_index("x") * NY + lax.axis_index("y"), lax.axis_index("zl"), lax.axis_index("zh"))


def body(positions, scales, onsite, probes):
    atoms = A * NX * NZL * NY
    probe_total = NP * NZH * NC
    strength = 4.0 / math.sqrt(atoms)
    scales, onsite = scales[None, :], onsite[None, :]
    sent = pack(positions, scales, onsite, probes)
    gathered = lax.all_to_all(sent, ("zl", "zh"), 0, 0, tiled=True)
    far = lax.all_to_all(line(gathered), ("x", "y"), 0, 0, tiled=True)
    steps = lax.all_to_all(step(place, strength, far), ("x", "y"), 0, 0, tiled=True)
    cheb, side = final(place, strength, far, steps, onsite, probes)
    sides = lax.all_gather(side, "c", axis=0, tiled=True)
    forces, energy = end(probe_total, sides)
    return cheb, forces, energy.reshape(())


def solution(mesh):
    fine = Mesh(mesh.devices.reshape(NX, NZL, NY, NZH, NC), ("x", "zl", "y", "zh", "c"))
    blk, probe = ("x", "zl", "y"), ("zh", "c")
    return jax.shard_map(
        body,
        mesh=fine,
        in_specs=(P(None, blk), P(blk), P(blk), P(None, probe, blk)),
        out_specs=(P(None, probe, blk), P(None, blk), P()),
        check_vma=False,
    )
```

```python
import math

import jax
import jax.numpy as jnp
from jax import lax
from jax.experimental import pallas as pl
from jax.experimental.pallas import tpu as pltpu
from jax.sharding import Mesh, PartitionSpec as P

SOFT_SQ = 0.25
F32 = jnp.float32
BF16 = jnp.bfloat16

NX, NZL, NY, NZH, NC = 4, 8, 4, 2, 2
PLANE = NX * NY
LINE = NZL * NZH
A = 32
NP = 16
CH = NZL * A
PR = NZH * NP
VEC = 3 * PR
ROWS = 2 * VEC + 16
HALF = CH // 2
VMEM = 48 * 1024 * 1024


def split3(value):
    hi = value.astype(BF16)
    rest = value - hi.astype(F32)
    mid = rest.astype(BF16)
    low = (rest - mid.astype(F32)).astype(BF16)
    return hi.astype(F32), mid.astype(F32), low.astype(F32)


def pack_kernel(pos_in, scale_in, onsite_in, probe_in, out_ref, pos_ref, scale_ref, onsite_ref, probe_ref, sems):
    pairs = ((pos_in, pos_ref), (scale_in, scale_ref), (onsite_in, onsite_ref), (probe_in, probe_ref))
    copies = [pltpu.make_async_copy(a, b, sems.at[k]) for k, (a, b) in enumerate(pairs)]
    for copy in copies:
        copy.start()
    for copy in copies:
        copy.wait()
    hi, mid, low = split3(onsite_ref[...])
    row = lax.broadcasted_iota(jnp.int32, (16, A), 0)
    meta = jnp.zeros((16, A), F32)
    pos = pos_ref[...].astype(F32)
    values = [pos[0:1], pos[1:2], pos[2:3], scale_ref[...].astype(F32), hi, mid, low]
    for k, value in enumerate(values):
        meta = jnp.where(row == k, jnp.broadcast_to(value, (16, A)), meta)
    parts = [probe_ref[c].astype(F32) for c in range(3)] + [meta]
    packet = jnp.concatenate(parts, axis=1).astype(BF16)
    for k in range(LINE):
        out_ref[k] = packet


def line_kernel(in_ref, out_ref):
    parts, values = [], []
    for first in (0, NZL // 2):
        lines = range(first, first + NZL // 2)
        for q in range(3):
            for zh in range(NZH):
                parts.append(jnp.concatenate(
                    [in_ref[zl * NZH + zh, :, q * A:(q + 1) * A] for zl in lines], axis=1))
        values.append(jnp.concatenate(
            [in_ref[zl * NZH, :, 3 * A:4 * A].astype(F32) for zl in lines], axis=1)[0:8])
    parts.append(jnp.concatenate(values, axis=0).astype(BF16))
    packet = jnp.concatenate(parts, axis=0)
    for k in range(PLANE):
        out_ref[k] = packet


def vectors_of(ref, k):
    return jnp.concatenate([ref[k, 0:VEC], ref[k, VEC:2 * VEC]], axis=1)


def values_of(ref, k):
    both = ref[k, 2 * VEC:ROWS].astype(F32)
    return jnp.concatenate([both[0:8], both[8:16]], axis=1)


def geometry(xi, yi, zi, si, xj, yj, zj, sj):
    rx, ry, rz = xi - xj, yi - yj, zi - zj
    q = lax.rsqrt(rx * rx + ry * ry + rz * rz + SOFT_SQ)
    q2 = q * q
    a = (si * sj) * (q2 * q)
    b = (3.0 * a) * q2
    return rx, ry, rz, q2, a, b


def tensor(rx, ry, rz, a, b):
    tx, ty, tz = rx * b, ry * b, rz * b
    return (tx * rx - a, tx * ry, tx * rz, ty * ry - a, ty * rz, tz * rz - a)


def doubled(xi, yi, zi, si, xj, yj, zj, sj):
    rx, ry, rz = xi - xj, yi - yj, zi - zj
    q = lax.rsqrt(rx * rx + ry * ry + rz * rz + 4.0 * SOFT_SQ)
    q2 = q * q
    a = (si * sj) * (q2 * q)
    b = (3.0 * a) * q2
    tx, ty = rx * b, ry * b
    xx, yy = tx * rx - a, ty * ry - a
    return (xx, tx * ry, tx * rz, yy, ty * rz, -b - (xx + yy))


NT = (((1,), (1,)), ((), ()))


def columns(vectors, values):
    rest = jnp.zeros((128 - VEC - values.shape[0], CH), F32)
    return jnp.concatenate([vectors.astype(F32), values, rest], axis=0).T


def step_kernel(ids, strength, far_ref, out_ref, even_ref, odd_ref, col_ref, acc_ref):
    own = ids()[0]
    values = values_of(far_ref, own)
    turned = columns(vectors_of(far_ref, own), values)
    for k in range(4):
        column = turned[:, VEC + k:VEC + k + 1]
        col_ref[k] = jnp.broadcast_to(column if k == 3 else 2.0 * column, (CH, 128))
    acc_ref[...] = jnp.zeros_like(acc_ref)
    sub = 16

    def build(jc, tile_ref):
        v = values_of(far_ref, jc)
        xj, yj, zj, sj = 2.0 * v[0:1], 2.0 * v[1:2], 2.0 * v[2:3], v[3:4] * (8.0 * strength)
        for i0 in range(0, CH, sub):
            rows = slice(i0, i0 + sub)
            near = [col_ref[k, rows] for k in range(4)]
            for half in range(2):
                lanes = slice(half * 128, half * 128 + 128)
                tile = doubled(*near, xj[:, lanes], yj[:, lanes], zj[:, lanes], sj[:, lanes])
                for k, value in enumerate(tile):
                    tile_ref[k, rows, lanes] = value.astype(BF16)

    def multiply(jc, tile_ref):
        vec = vectors_of(far_ref, jc)
        vx, vy, vz = vec[0:PR], vec[PR:2 * PR], vec[2 * PR:]

        def times(lhs, k):
            return lax.dot_general(lhs, tile_ref[k], NT, preferred_element_type=F32)

        xx, yy, zz = times(vx, 0), times(vy, 3), times(vz, 5)
        xy = times(vec[0:2 * PR], 1)
        yz = times(vec[PR:], 4)
        xz = times(jnp.concatenate([vx, vz], axis=0), 2)
        acc_ref[0:PR] += xx + xy[PR:] + xz[PR:]
        acc_ref[PR:2 * PR] += yy + xy[:PR] + yz[PR:]
        acc_ref[2 * PR:] += zz + xz[:PR] + yz[:PR]

    build(0, even_ref)

    def turn(jc, carry):
        @pl.when(lax.rem(jc, 2) == 0)
        def _():
            build(jc + 1, odd_ref)
            multiply(jc, even_ref)

        @pl.when((lax.rem(jc, 2) == 1) & (jc < PLANE - 1))
        def _():
            build(jc + 1, even_ref)
            multiply(jc, odd_ref)
        return carry

    lax.fori_loop(0, PLANE, turn, 0)
    multiply(PLANE - 1, odd_ref)
    onsite = values[4:5] + values[5:6] + values[6:7]
    z = vectors_of(far_ref, own).astype(F32)
    still = values[0:1] - values[0:1]
    pair = doubled(still, still, still, values[3:4], still, still, still, values[3:4] * (8.0 * strength))
    kept = [jnp.broadcast_to(pair[k].astype(BF16).astype(F32), (PR, CH)) for k in (0, 3, 5)]
    exact = onsite * z + (acc_ref[...] - jnp.concatenate(kept, axis=0) * z)
    step = exact.astype(BF16)
    w = step.astype(F32)
    part = 0.5 * (z - exact) * w + 0.25 * z * z
    total = jnp.sum(jnp.sum(part, axis=0, keepdims=True), axis=1, keepdims=True)
    pieces = split3(total)
    row = lax.broadcasted_iota(jnp.int32, (16, HALF), 0)
    extra = jnp.zeros((16, HALF), F32)
    for k in range(3):
        extra = jnp.where(row == k, jnp.broadcast_to(pieces[k], (16, HALF)), extra)
    result = jnp.concatenate([step[:, :HALF], step[:, HALF:], extra.astype(BF16)], axis=0)
    for k in range(PLANE):
        out_ref[k] = result


def transposed(value):
    return jnp.concatenate([value, jnp.zeros((128 - A, 128), F32)], axis=0).T


def final_kernel(ids, strength, far_ref, step_ref, onsite_ref, probe_ref, cheb_ref, side_ref, colz_ref, colw_ref):
    own, zl, zh = ids()
    colz_ref[...] = columns(vectors_of(far_ref, own), values_of(far_ref, own))
    colw_ref[...] = columns(vectors_of(step_ref, own), jnp.zeros((8, CH), F32))
    mine = pl.ds(pl.multiple_of(zl * A, A), A)
    zi, wi = colz_ref[mine], colw_ref[mine]
    near = [jnp.broadcast_to(zi[:, VEC + k:VEC + k + 1], (A, CH)) for k in range(4)]
    left = []
    for c in range(3):
        lanes = slice(c * PR, (c + 1) * PR)
        zc, wc = 0.5 * zi[:, lanes], -0.5 * wi[:, lanes]
        left.append(jnp.concatenate([zc, wc, -zc], axis=1))
    left = jnp.concatenate(left, axis=0).astype(BF16)
    row = lax.broadcasted_iota(jnp.int32, (A, CH), 0)
    lane = lax.broadcasted_iota(jnp.int32, (A, CH), 1)

    def chunk(jc, carry):
        gx, gy, gz, image, energy = carry
        meta = values_of(far_ref, jc)
        rx, ry, rz, q2, a, b = geometry(
            *near, meta[0:1], meta[1:2], meta[2:3], meta[3:4] * strength)
        same = row + (own * CH + zl * A) == lane + jc * CH
        xx, xy, xz, yy, yz, zz = tensor(rx, ry, rz, jnp.where(same, 0.0, a), b)
        z, w = vectors_of(far_ref, jc), vectors_of(step_ref, jc)
        kinds = ((xx, xy, xz), (xy, yy, yz), (xz, yz, zz))
        weight = []
        for d in range(3):
            rows = slice(d * PR, (d + 1) * PR)
            tile = jnp.concatenate(kinds[d], axis=0).astype(BF16)
            image = image + lax.dot_general(w[rows], tile, NT, preferred_element_type=F32)
            right = jnp.concatenate([z[rows], z[rows], w[rows]], axis=0)
            weight.append(jnp.dot(left, right, preferred_element_type=F32))

        def wt(c, d):
            return weight[d][c * A:(c + 1) * A]

        trace = wt(0, 0) + wt(1, 1) + wt(2, 2)
        sxy, sxz, syz = wt(0, 1) + wt(1, 0), wt(0, 2) + wt(2, 0), wt(1, 2) + wt(2, 1)
        ux = 2.0 * wt(0, 0) * rx + sxy * ry + sxz * rz
        uy = sxy * rx + 2.0 * wt(1, 1) * ry + syz * rz
        uz = sxz * rx + syz * ry + 2.0 * wt(2, 2) * rz
        radial = trace - 2.5 * q2 * (rx * ux + ry * uy + rz * uz)
        gx = gx + b * (ux + rx * radial)
        gy = gy + b * (uy + ry * radial)
        gz = gz + b * (uz + rz * radial)
        piece = step_ref[jc, 2 * VEC:ROWS].astype(F32)
        energy = energy + (piece[0:1] + piece[1:2] + piece[2:3])
        return gx, gy, gz, image, energy

    zero = jnp.zeros((A, CH), F32)
    gx, gy, gz, image, energy = lax.fori_loop(
        0, PLANE, chunk,
        (zero, zero, zero, jnp.zeros((PR, 3 * A), F32), jnp.zeros((1, HALF), F32)),
        unroll=16)
    w_rows = transposed(wi)
    for c in range(3):
        both = image[:, c * A:(c + 1) * A]
        w_both = w_rows[c * PR:(c + 1) * PR, 0:A]
        high = jnp.full((NP, A), zh, jnp.int32) > 0
        part = jnp.where(high, both[NP:], both[:NP])
        w = jnp.where(high, w_both[NP:], w_both[:NP])
        cheb_ref[c] = 2.0 * (onsite_ref[...] * w + part) - probe_ref[c].astype(F32)
    out = []
    for g in (gx, gy, gz):
        out.append(jnp.sum(transposed(g[:, 0:128] + g[:, 128:256]), axis=0, keepdims=True))
    out.append(energy)
    side = jnp.concatenate(out + [jnp.zeros((4, 128), F32)], axis=0)
    side_ref[...] = side


def spec():
    return pl.BlockSpec(memory_space=pltpu.VMEM)


def call(kernel, outs, scratch, operands):
    return pl.pallas_call(
        kernel,
        out_shape=outs,
        in_specs=[spec() for _ in operands],
        out_specs=jax.tree.map(lambda _: spec(), outs),
        scratch_shapes=scratch,
        compiler_params=pltpu.CompilerParams(vmem_limit_bytes=VMEM),
    )(*operands)


def pack(*operands):
    scratch = [pltpu.VMEM(x.shape, x.dtype) for x in operands] + [pltpu.SemaphoreType.DMA((4,))]
    return pl.pallas_call(
        pack_kernel,
        out_shape=jax.ShapeDtypeStruct((LINE, 16, 4 * A), BF16),
        in_specs=[pl.BlockSpec(memory_space=pltpu.HBM) for _ in operands],
        out_specs=spec(),
        scratch_shapes=scratch,
        compiler_params=pltpu.CompilerParams(vmem_limit_bytes=VMEM),
    )(*(pltpu.with_memory_space_constraint(x, pltpu.HBM) for x in operands))


def line(gathered):
    return call(line_kernel, jax.ShapeDtypeStruct((PLANE, ROWS, HALF), BF16), [], (gathered,))


def step(ids, strength, far):
    def kernel(*refs):
        step_kernel(ids, strength, *refs)
    scratch = [pltpu.VMEM((6, CH, CH), BF16), pltpu.VMEM((6, CH, CH), BF16), pltpu.VMEM((4, CH, 128), F32), pltpu.VMEM((VEC, CH), F32)]
    return call(kernel, jax.ShapeDtypeStruct((PLANE, ROWS, HALF), BF16), scratch, (far,))


def final(ids, strength, far, steps, onsite, probes):
    def kernel(*refs):
        final_kernel(ids, strength, *refs)
    outs = (jax.ShapeDtypeStruct((3, NP, A), F32), jax.ShapeDtypeStruct((8, 128), F32))
    scratch = [pltpu.VMEM((CH, 128), F32), pltpu.VMEM((CH, 128), F32)]
    return call(kernel, outs, scratch, (far, steps, onsite, probes))


def end_kernel(probe_total, side_ref, image_ref, cheb_ref, forces_ref, energy_ref):
    cheb_ref[...] = image_ref[...]
    both = side_ref[0:8] + side_ref[8:16]
    forces_ref[...] = (-2.0 / probe_total) * both[0:3, 0:A]
    energy_ref[...] = both[3:4, 0:1] / probe_total


def end(probe_total, sides, cheb):
    def kernel(*refs):
        end_kernel(probe_total, *refs)
    shapes = ((3, NP, A), (3, A), (1, 1))
    outs = tuple(jax.ShapeDtypeStruct(x, F32) for x in shapes)
    return call(kernel, outs, [], (sides, cheb))


def place():
    return (lax.axis_index("x") * NY + lax.axis_index("y"), lax.axis_index("zl"), lax.axis_index("zh"))


def body(positions, scales, onsite, probes):
    atoms = A * NX * NZL * NY
    probe_total = NP * NZH * NC
    strength = 4.0 / math.sqrt(atoms)
    scales, onsite = scales[None, :], onsite[None, :]
    sent = pack(positions, scales, onsite, probes)
    gathered = lax.all_to_all(sent, ("zl", "zh"), 0, 0, tiled=True)
    far = lax.all_to_all(line(gathered), ("x", "y"), 0, 0, tiled=True)
    steps = lax.all_to_all(step(place, strength, far), ("x", "y"), 0, 0, tiled=True)
    cheb, side = final(place, strength, far, steps, onsite, probes)
    sides = lax.all_gather(side, "c", axis=0, tiled=True)
    cheb, forces, energy = end(probe_total, sides, cheb)
    return cheb, forces, energy.reshape(())


def solution(mesh):
    fine = Mesh(mesh.devices.reshape(NX, NZL, NY, NZH, NC), ("x", "zl", "y", "zh", "c"))
    blk, probe = ("x", "zl", "y"), ("zh", "c")
    return jax.shard_map(
        body,
        mesh=fine,
        in_specs=(P(None, blk), P(blk), P(blk), P(None, probe, blk)),
        out_specs=(P(None, probe, blk), P(None, blk), P()),
        check_vma=False,
    )
```

```python
import math

import jax
import jax.numpy as jnp
from jax import lax
from jax.experimental import pallas as pl
from jax.experimental.pallas import tpu as pltpu
from jax.sharding import Mesh, PartitionSpec as P

SOFT_SQ = 0.25
F32 = jnp.float32
BF16 = jnp.bfloat16

NX, NZL, NY, NZH, NC = 4, 8, 4, 2, 2
PLANE = NX * NY
LINE = NZL * NZH
A = 32
NP = 16
CH = NZL * A
PR = NZH * NP
VEC = 3 * PR
ROWS = 2 * VEC + 16
HALF = CH // 2
VMEM = 48 * 1024 * 1024


def split3(value):
    hi = value.astype(BF16)
    rest = value - hi.astype(F32)
    mid = rest.astype(BF16)
    low = (rest - mid.astype(F32)).astype(BF16)
    return hi.astype(F32), mid.astype(F32), low.astype(F32)


def pack_kernel(pos_ref, scale_ref, onsite_ref, probe_ref, out_ref):
    hi, mid, low = split3(onsite_ref[...])
    row = lax.broadcasted_iota(jnp.int32, (16, A), 0)
    meta = jnp.zeros((16, A), F32)
    pos = pos_ref[...].astype(F32)
    values = [pos[0:1], pos[1:2], pos[2:3], scale_ref[...].astype(F32), hi, mid, low]
    for k, value in enumerate(values):
        meta = jnp.where(row == k, jnp.broadcast_to(value, (16, A)), meta)
    parts = [probe_ref[c].astype(F32) for c in range(3)] + [meta]
    packet = jnp.concatenate(parts, axis=1).astype(BF16)
    for k in range(LINE):
        out_ref[k] = packet


def line_kernel(in_ref, out_ref):
    parts, values = [], []
    for first in (0, NZL // 2):
        lines = range(first, first + NZL // 2)
        for q in range(3):
            for zh in range(NZH):
                parts.append(jnp.concatenate(
                    [in_ref[zl * NZH + zh, :, q * A:(q + 1) * A] for zl in lines], axis=1))
        values.append(jnp.concatenate(
            [in_ref[zl * NZH, :, 3 * A:4 * A].astype(F32) for zl in lines], axis=1)[0:8])
    parts.append(jnp.concatenate(values, axis=0).astype(BF16))
    packet = jnp.concatenate(parts, axis=0)
    for k in range(PLANE):
        out_ref[k] = packet


def vectors_of(ref, k):
    return jnp.concatenate([ref[k, 0:VEC], ref[k, VEC:2 * VEC]], axis=1)


def values_of(ref, k):
    both = ref[k, 2 * VEC:ROWS].astype(F32)
    return jnp.concatenate([both[0:8], both[8:16]], axis=1)


def geometry(xi, yi, zi, si, xj, yj, zj, sj):
    rx, ry, rz = xi - xj, yi - yj, zi - zj
    q = lax.rsqrt(rx * rx + ry * ry + rz * rz + SOFT_SQ)
    q2 = q * q
    a = (si * sj) * (q2 * q)
    b = (3.0 * a) * q2
    return rx, ry, rz, q2, a, b


def tensor(rx, ry, rz, a, b):
    tx, ty, tz = rx * b, ry * b, rz * b
    return (tx * rx - a, tx * ry, tx * rz, ty * ry - a, ty * rz, tz * rz - a)


def doubled(xi, yi, zi, si, xj, yj, zj, sj):
    rx, ry, rz = xi - xj, yi - yj, zi - zj
    q = lax.rsqrt(rx * rx + ry * ry + rz * rz + 4.0 * SOFT_SQ)
    q2 = q * q
    a = (si * sj) * (q2 * q)
    b = (3.0 * a) * q2
    tx, ty = rx * b, ry * b
    xx, yy = tx * rx - a, ty * ry - a
    return (xx, tx * ry, tx * rz, yy, ty * rz, -b - (xx + yy))


NT = (((1,), (1,)), ((), ()))


def columns(vectors, values):
    rest = jnp.zeros((128 - VEC - values.shape[0], CH), F32)
    return jnp.concatenate([vectors.astype(F32), values, rest], axis=0).T


def step_kernel(ids, strength, far_ref, out_ref, even_ref, odd_ref, col_ref, acc_ref):
    own = ids()[0]
    values = values_of(far_ref, own)
    turned = columns(vectors_of(far_ref, own), values)
    for k in range(4):
        column = turned[:, VEC + k:VEC + k + 1]
        col_ref[k] = jnp.broadcast_to(column if k == 3 else 2.0 * column, (CH, 128))
    acc_ref[...] = jnp.zeros_like(acc_ref)
    sub = 16

    def build(jc, tile_ref):
        v = values_of(far_ref, jc)
        xj, yj, zj, sj = 2.0 * v[0:1], 2.0 * v[1:2], 2.0 * v[2:3], v[3:4] * (8.0 * strength)
        for i0 in range(0, CH, sub):
            rows = slice(i0, i0 + sub)
            near = [col_ref[k, rows] for k in range(4)]
            for half in range(2):
                lanes = slice(half * 128, half * 128 + 128)
                tile = doubled(*near, xj[:, lanes], yj[:, lanes], zj[:, lanes], sj[:, lanes])
                for k, value in enumerate(tile):
                    tile_ref[k, rows, lanes] = value.astype(BF16)

    def multiply(jc, tile_ref):
        vec = vectors_of(far_ref, jc)
        vx, vy, vz = vec[0:PR], vec[PR:2 * PR], vec[2 * PR:]

        def times(lhs, k):
            return lax.dot_general(lhs, tile_ref[k], NT, preferred_element_type=F32)

        xx, yy, zz = times(vx, 0), times(vy, 3), times(vz, 5)
        xy = times(vec[0:2 * PR], 1)
        yz = times(vec[PR:], 4)
        xz = times(jnp.concatenate([vx, vz], axis=0), 2)
        acc_ref[0:PR] += xx + xy[PR:] + xz[PR:]
        acc_ref[PR:2 * PR] += yy + xy[:PR] + yz[PR:]
        acc_ref[2 * PR:] += zz + xz[:PR] + yz[:PR]

    build(0, even_ref)

    def turn(jc, carry):
        @pl.when(lax.rem(jc, 2) == 0)
        def _():
            build(jc + 1, odd_ref)
            multiply(jc, even_ref)

        @pl.when((lax.rem(jc, 2) == 1) & (jc < PLANE - 1))
        def _():
            build(jc + 1, even_ref)
            multiply(jc, odd_ref)
        return carry

    lax.fori_loop(0, PLANE, turn, 0)
    multiply(PLANE - 1, odd_ref)
    onsite = values[4:5] + values[5:6] + values[6:7]
    z = vectors_of(far_ref, own).astype(F32)
    still = values[0:1] - values[0:1]
    pair = doubled(still, still, still, values[3:4], still, still, still, values[3:4] * (8.0 * strength))
    kept = [jnp.broadcast_to(pair[k].astype(BF16).astype(F32), (PR, CH)) for k in (0, 3, 5)]
    exact = onsite * z + (acc_ref[...] - jnp.concatenate(kept, axis=0) * z)
    step = exact.astype(BF16)
    w = step.astype(F32)
    part = 0.5 * (z - exact) * w + 0.25 * z * z
    total = jnp.sum(jnp.sum(part, axis=0, keepdims=True), axis=1, keepdims=True)
    pieces = split3(total)
    row = lax.broadcasted_iota(jnp.int32, (16, HALF), 0)
    extra = jnp.zeros((16, HALF), F32)
    for k in range(3):
        extra = jnp.where(row == k, jnp.broadcast_to(pieces[k], (16, HALF)), extra)
    result = jnp.concatenate([step[:, :HALF], step[:, HALF:], extra.astype(BF16)], axis=0)
    for k in range(PLANE):
        out_ref[k] = result


def transposed(value):
    return jnp.concatenate([value, jnp.zeros((128 - A, 128), F32)], axis=0).T


def final_kernel(ids, strength, far_ref, step_ref, onsite_ref, probe_ref, cheb_ref, side_ref, colz_ref, colw_ref):
    own, zl, zh = ids()
    colz_ref[...] = columns(vectors_of(far_ref, own), values_of(far_ref, own))
    colw_ref[...] = columns(vectors_of(step_ref, own), jnp.zeros((8, CH), F32))
    mine = pl.ds(pl.multiple_of(zl * A, A), A)
    zi, wi = colz_ref[mine], colw_ref[mine]
    near = [jnp.broadcast_to(zi[:, VEC + k:VEC + k + 1], (A, CH)) for k in range(4)]
    left = []
    for c in range(3):
        lanes = slice(c * PR, (c + 1) * PR)
        zc, wc = 0.5 * zi[:, lanes], -0.5 * wi[:, lanes]
        left.append(jnp.concatenate([zc, wc, -zc], axis=1))
    left = jnp.concatenate(left, axis=0).astype(BF16)
    row = lax.broadcasted_iota(jnp.int32, (A, CH), 0)
    lane = lax.broadcasted_iota(jnp.int32, (A, CH), 1)

    def chunk(jc, carry):
        gx, gy, gz, image, energy = carry
        meta = values_of(far_ref, jc)
        rx, ry, rz, q2, a, b = geometry(
            *near, meta[0:1], meta[1:2], meta[2:3], meta[3:4] * strength)
        same = row + (own * CH + zl * A) == lane + jc * CH
        xx, xy, xz, yy, yz, zz = tensor(rx, ry, rz, jnp.where(same, 0.0, a), b)
        z, w = vectors_of(far_ref, jc), vectors_of(step_ref, jc)
        kinds = ((xx, xy, xz), (xy, yy, yz), (xz, yz, zz))
        weight = []
        for d in range(3):
            rows = slice(d * PR, (d + 1) * PR)
            tile = jnp.concatenate(kinds[d], axis=0).astype(BF16)
            image = image + lax.dot_general(w[rows], tile, NT, preferred_element_type=F32)
            right = jnp.concatenate([z[rows], z[rows], w[rows]], axis=0)
            weight.append(jnp.dot(left, right, preferred_element_type=F32))

        def wt(c, d):
            return weight[d][c * A:(c + 1) * A]

        trace = wt(0, 0) + wt(1, 1) + wt(2, 2)
        sxy, sxz, syz = wt(0, 1) + wt(1, 0), wt(0, 2) + wt(2, 0), wt(1, 2) + wt(2, 1)
        ux = 2.0 * wt(0, 0) * rx + sxy * ry + sxz * rz
        uy = sxy * rx + 2.0 * wt(1, 1) * ry + syz * rz
        uz = sxz * rx + syz * ry + 2.0 * wt(2, 2) * rz
        radial = trace - 2.5 * q2 * (rx * ux + ry * uy + rz * uz)
        gx = gx + b * (ux + rx * radial)
        gy = gy + b * (uy + ry * radial)
        gz = gz + b * (uz + rz * radial)
        piece = step_ref[jc, 2 * VEC:ROWS].astype(F32)
        energy = energy + (piece[0:1] + piece[1:2] + piece[2:3])
        return gx, gy, gz, image, energy

    zero = jnp.zeros((A, CH), F32)
    gx, gy, gz, image, energy = lax.fori_loop(
        0, PLANE, chunk,
        (zero, zero, zero, jnp.zeros((PR, 3 * A), F32), jnp.zeros((1, HALF), F32)),
        unroll=16)
    w_rows = transposed(wi)
    for c in range(3):
        both = image[:, c * A:(c + 1) * A]
        w_both = w_rows[c * PR:(c + 1) * PR, 0:A]
        high = jnp.full((NP, A), zh, jnp.int32) > 0
        part = jnp.where(high, both[NP:], both[:NP])
        w = jnp.where(high, w_both[NP:], w_both[:NP])
        cheb_ref[c] = 2.0 * (onsite_ref[...] * w + part) - probe_ref[c].astype(F32)
    out = []
    for g in (gx, gy, gz):
        out.append(jnp.sum(transposed(g[:, 0:128] + g[:, 128:256]), axis=0, keepdims=True))
    out.append(energy)
    side = jnp.concatenate(out + [jnp.zeros((4, 128), F32)], axis=0)
    side_ref[...] = side


def spec():
    return pl.BlockSpec(memory_space=pltpu.VMEM)


def call(kernel, outs, scratch, operands):
    return pl.pallas_call(
        kernel,
        out_shape=outs,
        in_specs=[spec() for _ in operands],
        out_specs=jax.tree.map(lambda _: spec(), outs),
        scratch_shapes=scratch,
        compiler_params=pltpu.CompilerParams(vmem_limit_bytes=VMEM),
    )(*operands)


def pack(*operands):
    return call(pack_kernel, jax.ShapeDtypeStruct((LINE, 16, 4 * A), BF16), [], operands)


def line(gathered):
    return call(line_kernel, jax.ShapeDtypeStruct((PLANE, ROWS, HALF), BF16), [], (gathered,))


def step(ids, strength, far):
    def kernel(*refs):
        step_kernel(ids, strength, *refs)
    scratch = [pltpu.VMEM((6, CH, CH), BF16), pltpu.VMEM((6, CH, CH), BF16), pltpu.VMEM((4, CH, 128), F32), pltpu.VMEM((VEC, CH), F32)]
    return call(kernel, jax.ShapeDtypeStruct((PLANE, ROWS, HALF), BF16), scratch, (far,))


def final(ids, strength, far, steps, onsite, probes):
    def kernel(*refs):
        final_kernel(ids, strength, *refs)
    outs = (jax.ShapeDtypeStruct((3, NP, A), F32), jax.ShapeDtypeStruct((8, 128), F32))
    scratch = [pltpu.VMEM((CH, 128), F32), pltpu.VMEM((CH, 128), F32)]
    return call(kernel, outs, scratch, (far, steps, onsite, probes))


def end_kernel(probe_total, side_ref, image_ref, cheb_ref, forces_ref, energy_ref):
    cheb_ref[...] = image_ref[...]
    both = side_ref[0:8] + side_ref[8:16]
    forces_ref[...] = (-2.0 / probe_total) * both[0:3, 0:A]
    energy_ref[...] = both[3:4, 0:1] / probe_total


def end(probe_total, sides, cheb):
    def kernel(*refs):
        end_kernel(probe_total, *refs)
    shapes = ((3, NP, A), (3, A), (1, 1))
    outs = tuple(jax.ShapeDtypeStruct(x, F32) for x in shapes)
    return call(kernel, outs, [], (sides, cheb))


def place():
    return (lax.axis_index("x") * NY + lax.axis_index("y"), lax.axis_index("zl"), lax.axis_index("zh"))


def body(positions, scales, onsite, probes):
    atoms = A * NX * NZL * NY
    probe_total = NP * NZH * NC
    strength = 4.0 / math.sqrt(atoms)
    scales, onsite = scales[None, :], onsite[None, :]
    sent = pack(positions, scales, onsite, probes)
    gathered = lax.all_to_all(sent, ("zl", "zh"), 0, 0, tiled=True)
    far = lax.all_to_all(line(gathered), ("x", "y"), 0, 0, tiled=True)
    steps = lax.all_to_all(step(place, strength, far), ("x", "y"), 0, 0, tiled=True)
    cheb, side = final(place, strength, far, steps, onsite, probes)
    sides = lax.all_gather(side, "c", axis=0, tiled=True)
    cheb, forces, energy = end(probe_total, sides, cheb)
    return cheb, forces, energy.reshape(())


def solution(mesh):
    fine = Mesh(mesh.devices.reshape(NX, NZL, NY, NZH, NC), ("x", "zl", "y", "zh", "c"))
    blk, probe = ("x", "zl", "y"), ("zh", "c")
    return jax.shard_map(
        body,
        mesh=fine,
        in_specs=(P(None, blk), P(blk), P(blk), P(None, probe, blk)),
        out_specs=(P(None, probe, blk), P(None, blk), P()),
        check_vma=False,
    )
```
